128 devices in a mesh: shell: 8 (over y, z_hi), blk: 16 (over z_lo, x, core).
Axes of the slice: x: 4, y: 4, z: 4 (z_hi: 2, z_lo: 2; z = z_hi * 2 + z_lo), core: 2. Of those that a mesh axis runs over, the one named last changes fastest.
Arguments:
- cotangent: float32 [2, 256, 256, 128], P(None, 'blk', 'shell'), may hold values from -6 to 6
- bessel: float32 [256, 128, 128], P('shell'), may hold values from -0.5 to 0.5
- cycle_index: int32 [2048], replicated, may hold values from 0 to 2048
- mode_order: int32 [256], replicated, may hold values from 0 to 255, each once
Outputs:
- shell_maps: bfloat16 [128, 2048, 4096], P('shell', 'blk')
The draws below stay inside these ranges and needn't reach their ends.
Inputs may be any that keep to these rules, and one draw needn't show every extreme that they name: `mode_order`: every slot names a different order. `cycle_index`: cycle numbers may repeat.
All inputs are finite; a program needn't handle non-finite values.
Results may differ from the reference program's by a relative error of at most 0.015.
Values may be sent and summed in bfloat16 or wider, within the bound.
A program may use at most 192 MiB of HBM per device.

```python
import math
import jax
import jax.numpy as jnp
from jax import lax

L = 256
M = 256
K = 128
SHELLS = 128
NSIDE = 1024
NPHI = 4096
R_DEV = 128
NR = 2048
N_BLK = 16


def with_ends(drawn, key, least, high):
    dims = drawn.shape
    place = [jax.random.randint(jax.random.fold_in(key, axis), (), 0, dims[axis]) for axis in range(len(dims))]
    drawn = drawn.at[tuple(place)].set(least)
    longest = dims.index(max(dims))
    place[longest] = (place[longest] + 1) % dims[longest]
    return drawn.at[tuple(place)].set(high)


def level_of(own_key, shape, cuts, least, largest):
    def one(dim, blocks):
        steps = jax.random.uniform(jax.random.fold_in(jax.random.fold_in(own_key, 6), dim), (blocks,), jnp.float32, least / len(cuts), largest / len(cuts))
        return jnp.repeat(jnp.exp(steps), shape[dim] // blocks).reshape((-1,) + (1,) * (len(shape) - dim - 1))

    level = one(*cuts[0])
    for cut in cuts[1:]:
        level = level * one(*cut)
    return level


def gaussian(key, extent, width, limit, cuts=(), held_as=jnp.bfloat16):
    result = width * jax.random.normal(key, extent, jnp.float32)
    if cuts:
        result = result * level_of(key, extent, cuts, -0.22, 0.18)
    return jnp.clip(result, -limit, limit).astype(held_as)


def setup_inputs(seed: int = 0) -> dict:
    streams_of = jax.random.split(jax.random.key(seed), 5)
    cotangent = gaussian(streams_of[0], (2, M, L, K), 1.0, 6.0, ((1, 16), (2, 8)), jnp.float32)
    bessel = gaussian(streams_of[1], (L, K, SHELLS), K ** -0.5, 0.5, ((0, 8),), jnp.float32)
    cycle_index = with_ends(jax.random.randint(streams_of[2], (NR,), 0, 2 * NSIDE + 1), jax.random.fold_in(streams_of[2], 1), 0, 2 * NSIDE).astype(jnp.int32)
    mode_order = jax.random.permutation(streams_of[3], M).astype(jnp.int32)
    return dict(cotangent=cotangent, bessel=bessel, cycle_index=cycle_index, mode_order=mode_order)


def legendre_table(orders, heights, degrees):
    order_int = orders[:, None]
    order_float = order_int.astype(jnp.float32)
    height = heights[None, :]
    log_start = 0.5 * (jnp.log((2.0 * order_float + 1.0) / (4.0 * math.pi)) + lax.lgamma(order_float + 0.5) - 0.5 * math.log(math.pi) - lax.lgamma(order_float + 1.0)) + 0.5 * order_float * jnp.log(1.0 - height * height)
    start_value = jnp.exp(log_start)

    def advance(carry, degree):
        previous, earlier = carry
        degree_float = degree.astype(jnp.float32)
        numer = jnp.maximum(4.0 * degree_float * degree_float - 1.0, 1.0)
        denom = jnp.maximum(degree_float * degree_float - order_float * order_float, 1.0)
        factor_a = jnp.sqrt(numer / denom)
        lower = degree_float - 1.0
        factor_b = jnp.sqrt(jnp.maximum(lower * lower - order_float * order_float, 0.0) / jnp.maximum(4.0 * lower * lower - 1.0, 1.0))
        recurred = factor_a * (height * previous - factor_b * earlier)
        value = jnp.where(degree < order_int, jnp.zeros_like(recurred), jnp.where(degree == order_int, start_value, recurred))
        return ((value, previous), value)
    zeros = jnp.zeros_like(start_value)
    _, table = lax.scan(advance, (zeros, zeros), jnp.arange(degrees, dtype=jnp.int32))
    return table

def rotate(field_arrays, orders, cycles):
    parity = (cycles + 1) % 2
    angle = (orders[:, None] * parity[None, :]).astype(jnp.float32) * (math.pi / NPHI)
    cosine = jnp.cos(angle)
    sine = jnp.sin(angle)
    real_part = field_arrays[:, 0] * cosine - field_arrays[:, 1] * sine
    imag_part = field_arrays[:, 0] * sine + field_arrays[:, 1] * cosine
    return jnp.stack([real_part, imag_part], axis=1)

def synthesis_table(mode_order):
    pixels = jnp.arange(NPHI, dtype=jnp.int32)
    phase_position = mode_order[:, None] * pixels[None, :] % NPHI
    angle = phase_position.astype(jnp.float32) * (2.0 * math.pi / NPHI)
    weight = (jnp.where(mode_order == 0, 1.0, 2.0) * (2.0 / L)).astype(jnp.float32)[:, None]
    return jnp.stack([weight * jnp.cos(angle), -weight * jnp.sin(angle)]).astype(jnp.bfloat16)

def reference(cotangent, bessel, cycle_index, mode_order):
    coeffs = jnp.einsum('cmlk,lks->cmls', cotangent, bessel, precision=lax.Precision.HIGHEST).astype(jnp.bfloat16)
    coefficient_real = coeffs.astype(jnp.float32)
    table = synthesis_table(mode_order).astype(jnp.float32)

    def cycle_block(cycles):
        heights = (2.0 * NSIDE - 2.0 * cycles.astype(jnp.float32)) / (3.0 * NSIDE)
        legendre_rows = legendre_table(mode_order, heights, L)
        field_arrays = jnp.einsum('pzh,ezpi->iezh', legendre_rows, coefficient_real, precision=lax.Precision.HIGHEST)
        rotated = rotate(field_arrays, mode_order, cycles).astype(jnp.bfloat16).astype(jnp.float32)
        maps = jnp.einsum('scmr,cmj->srj', rotated, table, precision=lax.Precision.HIGHEST)
        return maps.astype(jnp.bfloat16)
    blocks = lax.map(cycle_block, cycle_index.reshape(N_BLK, R_DEV))
    return jnp.transpose(blocks, (1, 0, 2, 3)).reshape(SHELLS, NR, NPHI)
```

```python
import math

import jax
import jax.numpy as jnp
import numpy as np
from jax import lax
from jax.experimental import pallas as pl
from jax.experimental.pallas import tpu as pltpu
from jax.sharding import PartitionSpec as P

L = 256
M = 256
NSIDE = 1024
NPHI = 4096
ROWS = 128
SH = 16
MB = 32
LC = 16


def start_norms():
    m = range(M)
    value = [
        0.5 * (math.log((2 * k + 1) / (4 * math.pi)) + math.lgamma(k + 0.5) - math.lgamma(0.5) - math.lgamma(k + 1.0))
        for k in m
    ]
    return np.broadcast_to(np.array(value, np.float32)[:, None], (M, ROWS))


def legendre_rows(cycles, start_ref, step_ref):
    x = (2.0 * NSIDE - 2.0 * cycles.astype(jnp.float32)) / (3.0 * NSIDE)
    degree = lax.broadcasted_iota(jnp.int32, (L, ROWS), 0).astype(jnp.float32)
    root = jnp.sqrt(jnp.maximum(4.0 * degree * degree - 1.0, 1.0))
    lower = degree - 1.0
    root_lower = jnp.sqrt(jnp.maximum(4.0 * lower * lower - 1.0, 1.0))
    start_ref[...] = root * x
    step_ref[...] = root / root_lower
    return jnp.log(1.0 - x * x)


def legendre_block(block, log_height, norm_ref, x_ref, step_ref, stage_ref, table_ref):
    first = block * MB
    groups = MB // 8
    sub = lax.broadcasted_iota(jnp.int32, (8, ROWS), 0)
    orders = [(first + 8 * g + sub) for g in range(groups)]
    order_f = [o.astype(jnp.float32) for o in orders]
    square = [o * o for o in order_f]
    start = [
        jnp.exp(norm_ref[pl.ds(pl.multiple_of(first + 8 * g, 8), 8), :] + 0.5 * order_f[g] * log_height)
        for g in range(groups)
    ]

    def clear(k, _):
        for i in range(MB):
            table_ref[first + i, pl.ds(pl.multiple_of(k * LC, LC), LC), :] = jnp.zeros((LC, ROWS), jnp.bfloat16)
        return 0

    lax.fori_loop(0, first // LC, clear, 0)

    def chunk(k, carry, starting):
        prev, earlier, root_prev = carry
        base = pl.multiple_of(k * LC, LC)
        for j in range(LC):
            degree = base + j
            degree_f = degree.astype(jnp.float32)
            x_row = x_ref[pl.ds(degree, 1), :]
            step_row = step_ref[pl.ds(degree, 1), :]
            new, root_new = [], []
            for g in range(groups):
                d = degree_f * degree_f - square[g]
                inv = lax.rsqrt(jnp.maximum(d, 1.0) if starting else d)
                value = inv * (x_row * prev[g] - (step_row * root_prev[g]) * earlier[g])
                if starting:
                    value = jnp.where(orders[g] == degree, start[g], value)
                stage_ref[pl.ds(8 * g * LC + j, 8, stride=LC), :] = value
                new.append(value)
                root_new.append(d * inv)
            earlier, prev, root_prev = prev, new, root_new
        for i in range(MB):
            table_ref[first + i, pl.ds(base, LC), :] = stage_ref[i * LC:(i + 1) * LC, :].astype(jnp.bfloat16)
        return prev, earlier, root_prev

    zeros = [jnp.zeros((8, ROWS), jnp.float32)] * groups
    carry = (zeros, zeros, zeros)
    lo = first // LC
    carry = lax.fori_loop(lo, lo + MB // LC, lambda k, c: chunk(k, c, True), carry)
    lax.fori_loop(lo + MB // LC, L // LC, lambda k, c: chunk(k, c, False), carry)


def turn_tables(cycles, cos_ref, sin_ref):
    odd = (lax.rem(cycles + 1, 2) == 1)
    order = lax.broadcasted_iota(jnp.int32, (M, ROWS), 0).astype(jnp.float32)
    a = order * (math.pi / NPHI)
    q = a * a
    cosine = 1.0 - q * (0.5 - q * (1.0 / 24 - q * (1.0 / 720)))
    sine = a * (1.0 - q * (1.0 / 6 - q * (1.0 / 120 - q * (1.0 / 5040))))
    cos_ref[...] = jnp.where(odd, cosine, 1.0)
    sin_ref[...] = jnp.where(odd, sine, 0.0)


def field_of(order, coeffs, table_ref, cos_ref, sin_ref):
    f = jnp.dot(coeffs, table_ref[order], preferred_element_type=jnp.float32)
    c = cos_ref[pl.ds(order, 1), :]
    s = sin_ref[pl.ds(order, 1), :]
    fr, fi = f[:SH], f[SH:]
    return (fr * c - fi * s).astype(jnp.bfloat16), (fr * s + fi * c).astype(jnp.bfloat16)


def fields_kernel(mode_ref, cyc_ref, norm_ref, coeff_ref, out_ref, x_ref, step_ref, stage_ref, table_ref, cos_ref, sin_ref):
    own = lax.axis_index("blk")
    cycles = cyc_ref[pl.ds(own, 1), :]
    log_height = legendre_rows(cycles, x_ref, step_ref)
    turn_tables(cycles, cos_ref, sin_ref)

    def block(k, _):
        legendre_block(k, log_height, norm_ref, x_ref, step_ref, stage_ref, table_ref)
        return 0

    lax.fori_loop(0, M // MB, block, 0)

    def slots(k, _):
        for u in range(8):
            t = k * 8 + u
            re, im = field_of(mode_ref[t], coeff_ref[t], table_ref, cos_ref, sin_ref)
            out_ref[t, :SH, :] = re
            out_ref[t, SH:, :] = im
        return 0

    lax.fori_loop(0, M // 8, slots, 0)


SPS = 2
JC = 512


def twiddles(tab_ref):
    half = M // 2
    for par in range(2):
        order = 2 * lax.broadcasted_iota(jnp.int32, (half, 128), 0) + par
        pixel = lax.broadcasted_iota(jnp.int32, (half, 128), 1)
        w = jnp.where(order == 0, 2.0 / L, 4.0 / L)
        angle = lax.rem(order * pixel, NPHI).astype(jnp.float32) * (2.0 * math.pi / NPHI)
        turn = lax.rem(order * 128, NPHI).astype(jnp.float32) * (2.0 * math.pi / NPHI)
        c, s = w * jnp.cos(angle), w * jnp.sin(angle)
        tc, ts = jnp.cos(turn), jnp.sin(turn)
        for j in range(NPHI // 2 // 128):
            tab_ref[par, :half, j * 128:(j + 1) * 128] = c.astype(jnp.bfloat16)
            tab_ref[par, half:, j * 128:(j + 1) * 128] = (-s).astype(jnp.bfloat16)
            c, s = c * tc - s * ts, s * tc + c * ts


def maps_kernel(mode_ref, f_ref, out_ref, g_ref, tab_ref):
    half = M // 2

    @pl.when(pl.program_id(0) == 0)
    def _():
        twiddles(tab_ref)

        def place(k, _):
            for u in range(8):
                t = k * 8 + u
                m = mode_ref[t]
                row = lax.rem(m, 2) * M + m // 2
                v = f_ref[t].astype(jnp.float32)
                g_ref[pl.ds(row, SH, stride=2 * M), :] = v[:SH]
                g_ref[pl.ds(row + half, SH, stride=2 * M), :] = v[SH:]
            return 0

        lax.fori_loop(0, M // 8, place, 0)

    first = pl.program_id(0) * SPS
    even, odd = [], []
    for i in range(SPS):
        base = pl.multiple_of((first + i) * 2 * M, 2 * M)
        even.append(g_ref[pl.ds(base, M), :].T.astype(jnp.bfloat16))
        odd.append(g_ref[pl.ds(base + M, M), :].T.astype(jnp.bfloat16))
    even = jnp.concatenate(even, axis=0)
    odd = jnp.concatenate(odd, axis=0)
    for j in range(0, NPHI // 2, JC):
        e = jnp.dot(even, tab_ref[0, :, j:j + JC], preferred_element_type=jnp.float32)
        o = jnp.dot(odd, tab_ref[1, :, j:j + JC], preferred_element_type=jnp.float32)
        p = (e + o).astype(jnp.bfloat16)
        q = (e - o).astype(jnp.bfloat16)
        for i in range(SPS):
            out_ref[i, :, j:j + JC] = p[i * ROWS:(i + 1) * ROWS]
            out_ref[i, :, NPHI // 2 + j:NPHI // 2 + j + JC] = q[i * ROWS:(i + 1) * ROWS]


def maps_call(mode_order, fields):
    return pl.pallas_call(
        maps_kernel,
        out_shape=jax.ShapeDtypeStruct((SH, ROWS, NPHI), jnp.bfloat16),
        grid_spec=pltpu.PrefetchScalarGridSpec(
            num_scalar_prefetch=1,
            grid=(SH // SPS,),
            in_specs=[pl.BlockSpec((M, 2 * SH, ROWS), lambda i, m: (0, 0, 0))],
            out_specs=pl.BlockSpec((SPS, ROWS, NPHI), lambda i, m: (i, 0, 0)),
            scratch_shapes=[
                pltpu.VMEM((SH * 2 * M, ROWS), jnp.float32),
                pltpu.VMEM((2, M, NPHI // 2), jnp.bfloat16),
            ],
        ),
        compiler_params=pltpu.CompilerParams(vmem_limit_bytes=40 << 20),
        name="maps",
    )(mode_order, fields)


def fields_call(mode_order, cycle_index, coeffs):
    vmem = pl.BlockSpec(memory_space=pltpu.VMEM)
    return pl.pallas_call(
        fields_kernel,
        out_shape=jax.ShapeDtypeStruct((M, 2 * SH, ROWS), jnp.bfloat16),
        in_specs=[pl.BlockSpec(memory_space=pltpu.SMEM), vmem, vmem, vmem],
        out_specs=vmem,
        scratch_shapes=[
            pltpu.VMEM((L, ROWS), jnp.float32),
            pltpu.VMEM((L, ROWS), jnp.float32),
            pltpu.VMEM((MB * LC, ROWS), jnp.float32),
            pltpu.VMEM((M, L, ROWS), jnp.bfloat16),
            pltpu.VMEM((M, ROWS), jnp.float32),
            pltpu.VMEM((M, ROWS), jnp.float32),
        ],
        compiler_params=pltpu.CompilerParams(vmem_limit_bytes=50 << 20),
        name="fields",
    )(mode_order, cycle_index.reshape(-1, ROWS), jnp.asarray(start_norms()), coeffs)


def per_device(cotangent, bessel, cycle_index, mode_order):
    coeffs = jnp.einsum("cmlk,lks->cmls", cotangent, bessel).astype(jnp.bfloat16)
    coeffs = lax.all_to_all(coeffs, "shell", split_axis=3, concat_axis=2, tiled=True)
    coeffs = jnp.transpose(coeffs, (1, 0, 3, 2)).reshape(-1, 2 * SH, L)
    coeffs = lax.all_gather(coeffs, "blk", axis=0, tiled=True)
    return maps_call(mode_order, fields_call(mode_order, cycle_index, coeffs))


def solution(mesh):
    return jax.shard_map(
        per_device,
        mesh=mesh,
        in_specs=(P(None, "blk", "shell", None), P("shell", None, None), P(), P()),
        out_specs=P("shell", "blk", None),
        check_vma=False,
    )
```

```python
import math

import jax
import jax.numpy as jnp
import numpy as np
from jax import lax
from jax.experimental import pallas as pl
from jax.experimental.pallas import tpu as pltpu
from jax.sharding import PartitionSpec as P

L = 256
M = 256
NSIDE = 1024
NPHI = 4096
ROWS = 128
SH = 16
MB = 32
LC = 16


def start_norms():
    m = range(M)
    value = [
        0.5 * (math.log((2 * k + 1) / (4 * math.pi)) + math.lgamma(k + 0.5) - math.lgamma(0.5) - math.lgamma(k + 1.0))
        for k in m
    ]
    return np.broadcast_to(np.array(value, np.float32)[:, None], (M, ROWS))


def legendre_rows(cycles, start_ref, step_ref):
    x = (2.0 * NSIDE - 2.0 * cycles.astype(jnp.float32)) / (3.0 * NSIDE)
    degree = lax.broadcasted_iota(jnp.int32, (L, ROWS), 0).astype(jnp.float32)
    root = jnp.sqrt(jnp.maximum(4.0 * degree * degree - 1.0, 1.0))
    lower = degree - 1.0
    root_lower = jnp.sqrt(jnp.maximum(4.0 * lower * lower - 1.0, 1.0))
    start_ref[...] = root * x
    step_ref[...] = root / root_lower
    return jnp.log(1.0 - x * x)


def legendre_block(block, log_height, norm_ref, x_ref, step_ref, stage_ref, table_ref):
    first = block * MB
    groups = MB // 8
    sub = lax.broadcasted_iota(jnp.int32, (8, ROWS), 0)
    orders = [(first + 8 * g + sub) for g in range(groups)]
    order_f = [o.astype(jnp.float32) for o in orders]
    square = [o * o for o in order_f]
    start = [
        jnp.exp(norm_ref[pl.ds(pl.multiple_of(first + 8 * g, 8), 8), :] + 0.5 * order_f[g] * log_height)
        for g in range(groups)
    ]

    def clear(k, _):
        for i in range(MB):
            table_ref[first + i, pl.ds(pl.multiple_of(k * LC, LC), LC), :] = jnp.zeros((LC, ROWS), jnp.bfloat16)
        return 0

    lax.fori_loop(0, first // LC, clear, 0)

    def chunk(k, carry, starting):
        prev, earlier, root_prev = carry
        base = pl.multiple_of(k * LC, LC)
        for j in range(LC):
            degree = base + j
            degree_f = degree.astype(jnp.float32)
            x_row = x_ref[pl.ds(degree, 1), :]
            step_row = step_ref[pl.ds(degree, 1), :]
            new, root_new = [], []
            for g in range(groups):
                d = degree_f * degree_f - square[g]
                inv = lax.rsqrt(jnp.maximum(d, 1.0) if starting else d)
                value = inv * (x_row * prev[g] - (step_row * root_prev[g]) * earlier[g])
                if starting:
                    value = jnp.where(orders[g] == degree, start[g], value)
                stage_ref[pl.ds(8 * g * LC + j, 8, stride=LC), :] = value
                new.append(value)
                root_new.append(d * inv)
            earlier, prev, root_prev = prev, new, root_new
        for i in range(MB):
            table_ref[first + i, pl.ds(base, LC), :] = stage_ref[i * LC:(i + 1) * LC, :].astype(jnp.bfloat16)
        return prev, earlier, root_prev

    zeros = [jnp.zeros((8, ROWS), jnp.float32)] * groups
    carry = (zeros, zeros, zeros)
    lo = first // LC
    carry = lax.fori_loop(lo, lo + MB // LC, lambda k, c: chunk(k, c, True), carry)
    lax.fori_loop(lo + MB // LC, L // LC, lambda k, c: chunk(k, c, False), carry)


def turn_tables(cycles, cos_ref, sin_ref):
    odd = (lax.rem(cycles + 1, 2) == 1)
    order = lax.broadcasted_iota(jnp.int32, (M, ROWS), 0).astype(jnp.float32)
    a = order * (math.pi / NPHI)
    q = a * a
    cosine = 1.0 - q * (0.5 - q * (1.0 / 24 - q * (1.0 / 720)))
    sine = a * (1.0 - q * (1.0 / 6 - q * (1.0 / 120 - q * (1.0 / 5040))))
    cos_ref[...] = jnp.where(odd, cosine, 1.0)
    sin_ref[...] = jnp.where(odd, sine, 0.0)


def field_of(order, coeffs, table_ref, cos_ref, sin_ref):
    f = jnp.dot(coeffs, table_ref[order], preferred_element_type=jnp.float32)
    c = cos_ref[pl.ds(order, 1), :]
    s = sin_ref[pl.ds(order, 1), :]
    fr, fi = f[:SH], f[SH:]
    return (fr * c - fi * s).astype(jnp.bfloat16), (fr * s + fi * c).astype(jnp.bfloat16)


GROUP = 8
KL = L // GROUP
SLOTS = 16
HALF = SLOTS // 2
WAVES = 128
MESH = pl.DeviceIdType.MESH


def radial(cot_ref, bes_ref, stage_ref, send_ref):
    def degree(k, _):
        for u in range(4):
            l = k * 4 + u
            c = cot_ref[pl.ds(l, 2 * SLOTS, stride=KL), :].astype(jnp.bfloat16)
            w = bes_ref[pl.ds(pl.multiple_of(l * WAVES, WAVES), WAVES), :].astype(jnp.bfloat16)
            stage_ref[pl.ds(l, 2 * SLOTS, stride=KL), :] = jnp.dot(c, w, preferred_element_type=jnp.float32)
        return 0

    lax.fori_loop(0, KL // 4, degree, 0)
    for q in range(8):
        tile = stage_ref[q * 128:(q + 1) * 128, :].T.astype(jnp.bfloat16)
        for h in range(GROUP):
            send_ref[h, q] = tile[h * SH:(h + 1) * SH]


def shuffle_matrix(perm_ref):
    k = lax.broadcasted_iota(jnp.int32, (512, 512), 0)
    n = lax.broadcasted_iota(jnp.int32, (512, 512), 1)
    to = lax.rem(k, 128) // 32 * 128 + k // 128 * 32 + lax.rem(k, 32)
    perm_ref[...] = (to == n).astype(jnp.float32).astype(jnp.bfloat16)


def relayout(recv_ref, perm_ref, own, block_ref):
    for h in range(2):
        x = jnp.concatenate([recv_ref[4 * h + j].reshape(128, 128) for j in range(4)], axis=1)
        y = jnp.dot(x, perm_ref[...], preferred_element_type=jnp.float32).astype(jnp.bfloat16)
        for q in range(8):
            for i in range(4):
                c, t = divmod(4 * q + i, SLOTS)
                block_ref[own, t, c * SH:(c + 1) * SH, h * 128:(h + 1) * 128] = y[q * SH:(q + 1) * SH, i * 128:(i + 1) * 128]


def fields_kernel(
    mode_ref, cyc_ref, norm_ref, cot_hbm, bes_hbm, out_ref,
    x_ref, step_ref, stage_ref, table_ref, cos_ref, sin_ref,
    cot_ref, bes_ref, rad_ref, send_ref, recv_ref, perm_ref, block_ref,
    load_sem, a2a_send, a2a_recv, ring_send, ring_recv,
):
    own = lax.axis_index("blk")
    shell = lax.axis_index("shell")
    core = lax.rem(own, 2)
    x = lax.rem(own // 2, 4)
    z = own // 8
    d = 1 - 2 * core

    def at(dz, k):
        return lax.rem(z + dz, 2) * 8 + lax.rem(x + k * d + 8, 4) * 2 + core

    ahead, behind, across, sibling = at(0, 1), at(0, -1), at(1, 0), own + d

    loads = [
        pltpu.make_async_copy(cot_hbm, cot_ref, load_sem.at[0]),
        pltpu.make_async_copy(bes_hbm, bes_ref, load_sem.at[1]),
    ]
    for copy in loads:
        copy.start()
    barrier = pltpu.get_barrier_semaphore()
    for peer in (ahead, behind, across, sibling):
        pl.semaphore_signal(barrier, inc=1, device_id={"blk": peer}, device_id_type=MESH)
    for k in range(1, GROUP):
        pl.semaphore_signal(barrier, inc=1, device_id={"shell": lax.rem(shell + k, GROUP)}, device_id_type=MESH)

    cycles = cyc_ref[pl.ds(own, 1), :]
    log_height = legendre_rows(cycles, x_ref, step_ref)
    turn_tables(cycles, cos_ref, sin_ref)
    shuffle_matrix(perm_ref)

    def table(lo, hi):
        def block(k, _):
            legendre_block(k, log_height, norm_ref, x_ref, step_ref, stage_ref, table_ref)
            return 0

        lax.fori_loop(lo, hi, block, 0)

    for copy in loads:
        copy.wait()
    radial(cot_ref, bes_ref, rad_ref, send_ref)
    pl.semaphore_wait(barrier, 4 + GROUP - 1)
    exchange = []
    for k in range(1, GROUP):
        to = lax.rem(shell + k, GROUP)
        copy = pltpu.make_async_remote_copy(
            src_ref=send_ref.at[to], dst_ref=recv_ref.at[shell], send_sem=a2a_send.at[k - 1], recv_sem=a2a_recv.at[k - 1],
            device_id={"shell": to}, device_id_type=MESH,
        )
        copy.start()
        exchange.append(copy)
    recv_ref[shell] = send_ref[shell]
    table(0, 1)
    for k in range(1, GROUP):
        source = lax.rem(shell - k + GROUP, GROUP)
        pltpu.make_async_remote_copy(
            src_ref=send_ref.at[source], dst_ref=recv_ref.at[source], send_sem=a2a_send.at[k - 1], recv_sem=a2a_recv.at[k - 1],
            device_id={"shell": source}, device_id_type=MESH,
        ).wait_recv()
    relayout(recv_ref, perm_ref, own, block_ref)

    sent = []

    def piece(part, index):
        return block_ref.at[index, pl.ds(HALF * part, HALF)]

    def describe(part, index, to, slot):
        return pltpu.make_async_remote_copy(
            src_ref=piece(part, index), dst_ref=piece(part, index), send_sem=ring_send.at[slot],
            recv_sem=ring_recv.at[part, index], device_id={"blk": to}, device_id_type=MESH,
        )

    def send(part, index, *targets):
        for to in targets:
            copy = describe(part, index, to, len(sent))
            copy.start()
            sent.append(copy)

    def arrive(part, index):
        describe(part, index, sibling, 0).wait_recv()

    for part in range(2):
        send(part, own, across, ahead, behind)
    for part in range(2):
        send(part, own, sibling)
    table(1, 2)
    arrive(0, at(1, 0))
    send(0, at(1, 0), ahead, behind)
    arrive(0, at(0, -1))
    send(0, at(0, -1), ahead)
    arrive(0, at(0, 1))
    for index in (at(1, 0), at(0, -1), at(0, 1)):
        send(0, index, sibling)
    table(2, 3)
    arrive(1, at(0, -1))
    send(1, at(0, -1), ahead, across)
    arrive(1, at(0, 1))
    send(1, at(0, 1), across)
    for index in (at(0, -1), at(0, 1)):
        send(1, index, sibling)
    table(3, 5)
    arrive(0, at(1, -1))
    send(0, at(1, -1), ahead)
    arrive(1, at(0, 2))
    send(1, at(0, 2), across)
    arrive(0, at(0, 2))
    arrive(0, at(1, 1))
    for part, index in ((0, at(1, -1)), (1, at(0, 2)), (0, at(0, 2)), (0, at(1, 1))):
        send(part, index, sibling)
    table(5, 8)

    def slots(index, part):
        def step(k, _):
            for u in range(4):
                t = HALF * part + k * 4 + u
                g = index * SLOTS + t
                re, im = field_of(mode_ref[g], block_ref[index, t], table_ref, cos_ref, sin_ref)
                out_ref[g, :SH, :] = re
                out_ref[g, SH:, :] = im
            return 0

        lax.fori_loop(0, HALF // 4, step, 0)

    ready = [(0, own), (1, own)]
    ready += [(0, at(1, 0)), (0, at(0, -1)), (0, at(0, 1)), (1, at(0, -1)), (1, at(0, 1))]
    ready += [(0, at(1, -1)), (1, at(0, 2)), (0, at(0, 2)), (0, at(1, 1))]
    last = [(1, at(1, 0)), (1, at(1, -1)), (1, at(1, 1)), (0, at(1, 2)), (1, at(1, 2))]
    for part, index in last:
        arrive(part, index)
        send(part, index, sibling)
    for part, index in ready + last:
        slots(index, part)
    for part, index in ready + last:
        arrive(part, index + d)
        slots(index + d, part)
    for copy in exchange + sent:
        copy.wait_send()


SPS = 2
JC = 512


def twiddles(tab_ref):
    half = M // 2
    for par in range(2):
        order = 2 * lax.broadcasted_iota(jnp.int32, (half, 128), 0) + par
        pixel = lax.broadcasted_iota(jnp.int32, (half, 128), 1)
        w = jnp.where(order == 0, 2.0 / L, 4.0 / L)
        angle = lax.rem(order * pixel, NPHI).astype(jnp.float32) * (2.0 * math.pi / NPHI)
        turn = lax.rem(order * 128, NPHI).astype(jnp.float32) * (2.0 * math.pi / NPHI)
        c, s = w * jnp.cos(angle), w * jnp.sin(angle)
        tc, ts = jnp.cos(turn), jnp.sin(turn)
        for j in range(NPHI // 2 // 128):
            tab_ref[par, :half, j * 128:(j + 1) * 128] = c.astype(jnp.bfloat16)
            tab_ref[par, half:, j * 128:(j + 1) * 128] = (-s).astype(jnp.bfloat16)
            c, s = c * tc - s * ts, s * tc + c * ts


def maps_kernel(mode_ref, f_ref, out_ref, g_ref, tab_ref):
    half = M // 2

    @pl.when(pl.program_id(0) == 0)
    def _():
        twiddles(tab_ref)

        def place(k, _):
            for u in range(8):
                t = k * 8 + u
                m = mode_ref[t]
                row = lax.rem(m, 2) * M + m // 2
                v = f_ref[t].astype(jnp.float32)
                g_ref[pl.ds(row, SH, stride=2 * M), :] = v[:SH]
                g_ref[pl.ds(row + half, SH, stride=2 * M), :] = v[SH:]
            return 0

        lax.fori_loop(0, M // 8, place, 0)

    first = pl.program_id(0) * SPS
    even, odd = [], []
    for i in range(SPS):
        base = pl.multiple_of((first + i) * 2 * M, 2 * M)
        even.append(g_ref[pl.ds(base, M), :].T.astype(jnp.bfloat16))
        odd.append(g_ref[pl.ds(base + M, M), :].T.astype(jnp.bfloat16))
    even = jnp.concatenate(even, axis=0)
    odd = jnp.concatenate(odd, axis=0)
    for j in range(0, NPHI // 2, JC):
        e = jnp.dot(even, tab_ref[0, :, j:j + JC], preferred_element_type=jnp.float32)
        o = jnp.dot(odd, tab_ref[1, :, j:j + JC], preferred_element_type=jnp.float32)
        p = (e + o).astype(jnp.bfloat16)
        q = (e - o).astype(jnp.bfloat16)
        for i in range(SPS):
            out_ref[i, :, j:j + JC] = p[i * ROWS:(i + 1) * ROWS]
            out_ref[i, :, NPHI // 2 + j:NPHI // 2 + j + JC] = q[i * ROWS:(i + 1) * ROWS]


def maps_call(mode_order, fields):
    return pl.pallas_call(
        maps_kernel,
        out_shape=jax.ShapeDtypeStruct((SH, ROWS, NPHI), jnp.bfloat16),
        grid_spec=pltpu.PrefetchScalarGridSpec(
            num_scalar_prefetch=1,
            grid=(SH // SPS,),
            in_specs=[pl.BlockSpec((M, 2 * SH, ROWS), lambda i, m: (0, 0, 0))],
            out_specs=pl.BlockSpec((SPS, ROWS, NPHI), lambda i, m: (i, 0, 0)),
            scratch_shapes=[
                pltpu.VMEM((SH * 2 * M, ROWS), jnp.float32),
                pltpu.VMEM((2, M, NPHI // 2), jnp.bfloat16),
            ],
        ),
        compiler_params=pltpu.CompilerParams(vmem_limit_bytes=40 << 20),
        name="maps",
    )(mode_order, fields)


def fields_call(cotangent, bessel, cycle_index, mode_order):
    vmem = pl.BlockSpec(memory_space=pltpu.VMEM)
    hbm = pl.BlockSpec(memory_space=pl.ANY)
    return pl.pallas_call(
        fields_kernel,
        out_shape=jax.ShapeDtypeStruct((M, 2 * SH, ROWS), jnp.bfloat16),
        in_specs=[pl.BlockSpec(memory_space=pltpu.SMEM), vmem, vmem, hbm, hbm],
        out_specs=vmem,
        scratch_shapes=[
            pltpu.VMEM((L, ROWS), jnp.float32),
            pltpu.VMEM((L, ROWS), jnp.float32),
            pltpu.VMEM((MB * LC, ROWS), jnp.float32),
            pltpu.VMEM((M, L, ROWS), jnp.bfloat16),
            pltpu.VMEM((M, ROWS), jnp.float32),
            pltpu.VMEM((M, ROWS), jnp.float32),
            pltpu.VMEM((2 * SLOTS * KL, WAVES), jnp.float32),
            pltpu.VMEM((KL * WAVES, 128), jnp.float32),
            pltpu.VMEM((2 * SLOTS * KL, 128), jnp.float32),
            pltpu.VMEM((GROUP, 8, SH, 128), jnp.bfloat16),
            pltpu.VMEM((GROUP, 8, SH, 128), jnp.bfloat16),
            pltpu.VMEM((512, 512), jnp.bfloat16),
            pltpu.VMEM((16, SLOTS, 2 * SH, L), jnp.bfloat16),
            pltpu.SemaphoreType.DMA((2,)),
            pltpu.SemaphoreType.DMA((GROUP - 1,)),
            pltpu.SemaphoreType.DMA((GROUP - 1,)),
            pltpu.SemaphoreType.DMA((30,)),
            pltpu.SemaphoreType.DMA((2, 16)),
        ],
        compiler_params=pltpu.CompilerParams(vmem_limit_bytes=50 << 20, collective_id=0, has_side_effects=True),
        name="fields",
    )(
        mode_order, cycle_index.reshape(-1, ROWS), jnp.asarray(start_norms()),
        cotangent.reshape(-1, WAVES), bessel.reshape(-1, 128),
    )


def per_device(cotangent, bessel, cycle_index, mode_order):
    fields = fields_call(cotangent, bessel, cycle_index, mode_order)
    return maps_call(mode_order, fields)


def solution(mesh):
    return jax.shard_map(
        per_device,
        mesh=mesh,
        in_specs=(P(None, "blk", "shell", None), P("shell", None, None), P(), P()),
        out_specs=P("shell", "blk", None),
        check_vma=False,
    )
```

```python
import math

import jax
import jax.numpy as jnp
import numpy as np
from jax import lax
from jax.experimental import pallas as pl
from jax.experimental.pallas import tpu as pltpu
from jax.sharding import PartitionSpec as P

L = 256
M = 256
NSIDE = 1024
NPHI = 4096
ROWS = 128
SH = 16
LB = 64
GROUP = 8
KL = L // GROUP
SLOTS = 16
HALF = SLOTS // 2
WAVES = 128
MESH = pl.DeviceIdType.MESH


def start_norms():
    value = [
        0.5 * (math.log((2 * k + 1) / (4 * math.pi)) + math.lgamma(k + 0.5) - math.lgamma(0.5) - math.lgamma(k + 1.0))
        for k in range(M)
    ]
    table = np.zeros((M, ROWS), np.float32)
    table[:, 0] = value
    return table


def legendre_block(block, log_height, slope, norm_ref, table_ref):
    base = block * LB
    degree = base + lax.broadcasted_iota(jnp.int32, (LB, ROWS), 0)
    degree_f = degree.astype(jnp.float32)
    square = degree_f * (degree_f + 1.0)
    start = jnp.exp(norm_ref[base:base + LB, 0:1] + 0.5 * degree_f * log_height)
    unroll = 8

    def clear(i, _):
        for u in range(unroll):
            table_ref[base + LB + i * unroll + u, base:base + LB, :] = jnp.zeros((LB, ROWS), jnp.bfloat16)
        return 0

    lax.fori_loop(0, (M - LB - base) // unroll, clear, 0)

    def descend(first, count, carry, starting):
        def steps(i, carry):
            p, above, root = carry
            for u in range(unroll):
                m = first - 1 - (i * unroll + u)
                upper = (m + 1).astype(jnp.float32)
                e = square - upper * (upper - 1.0)
                inv = lax.rsqrt(jnp.maximum(e, 1.0) if starting else e)
                value = inv * ((upper * slope) * p - root * above)
                if starting:
                    value = jnp.where(degree == m, start, value)
                table_ref[m, base:base + LB, :] = value.astype(jnp.bfloat16)
                above, p, root = p, value, e * inv
            return p, above, root

        return lax.fori_loop(0, count // unroll, steps, carry)

    zero = jnp.zeros((LB, ROWS), jnp.float32)
    carry = descend(base + LB, LB, (zero, zero, zero), True)
    if base:
        descend(base, base, carry, False)


def turn_tables(cycles, cos_ref, sin_ref):
    odd = (lax.rem(cycles + 1, 2) == 1)
    order = lax.broadcasted_iota(jnp.int32, (M, ROWS), 0).astype(jnp.float32)
    a = order * (math.pi / NPHI)
    q = a * a
    cosine = 1.0 - q * (0.5 - q * (1.0 / 24 - q * (1.0 / 720)))
    sine = a * (1.0 - q * (1.0 / 6 - q * (1.0 / 120 - q * (1.0 / 5040))))
    cos_ref[...] = jnp.where(odd, cosine, 1.0)
    sin_ref[...] = jnp.where(odd, sine, 0.0)


def field_of(order, coeffs, table_ref, cos_ref, sin_ref):
    f = jnp.dot(coeffs, table_ref[order], preferred_element_type=jnp.float32)
    c = cos_ref[pl.ds(order, 1), :]
    s = sin_ref[pl.ds(order, 1), :]
    fr, fi = f[:SH], f[SH:]
    return (fr * c - fi * s).astype(jnp.bfloat16), (fr * s + fi * c).astype(jnp.bfloat16)


def radial(cot_ref, bes_ref, stage_ref, send_ref):
    def degree(k, _):
        for u in range(8):
            l = k * 8 + u
            c = cot_ref[pl.ds(l, 2 * SLOTS, stride=KL), :].astype(jnp.bfloat16)
            w = bes_ref[pl.ds(pl.multiple_of(l * WAVES, WAVES), WAVES), :].astype(jnp.bfloat16)
            stage_ref[pl.ds(l, 2 * SLOTS, stride=KL), :] = jnp.dot(c, w, preferred_element_type=jnp.float32)
        return 0

    lax.fori_loop(0, KL // 8, degree, 0)
    for q in range(8):
        tile = stage_ref[q * 128:(q + 1) * 128, :].T.astype(jnp.bfloat16)
        for h in range(GROUP):
            send_ref[h, q] = tile[h * SH:(h + 1) * SH]


def shuffle_matrix(perm_ref):
    k = lax.broadcasted_iota(jnp.int32, (512, 512), 0)
    n = lax.broadcasted_iota(jnp.int32, (512, 512), 1)
    to = ((k & 96) << 2) | ((k & 384) >> 2) | (k & 31)
    perm_ref[...] = jnp.where(to == n, 1.0, 0.0).astype(jnp.bfloat16)


def twiddles(tab_ref):
    half = M // 2
    rows = 32

    def part(index, _):
        par, first = lax.rem(index, 2), index // 2 * rows
        lane = lax.broadcasted_iota(jnp.int32, (rows, 128), 1)
        m = 2 * (first + lax.broadcasted_iota(jnp.int32, (rows, 128), 0)) + par
        a = m.astype(jnp.float32) * (2.0 * math.pi / NPHI)
        q = a * a
        tc = 1.0 - q * (0.5 - q * (1.0 / 24 - q * (1.0 / 720 - q * (1.0 / 40320))))
        ts = a * (1.0 - q * (1.0 / 6 - q * (1.0 / 120 - q * (1.0 / 5040 - q * (1.0 / 362880)))))
        c, s = jnp.where(m == 0, 2.0 / L, 4.0 / L), jnp.zeros((rows, 128), jnp.float32)
        for b in range(7):
            on = (lane & (1 << b)) != 0
            c, s = jnp.where(on, c * tc - s * ts, c), jnp.where(on, s * tc + c * ts, s)
            tc, ts = tc * tc - ts * ts, 2.0 * tc * ts
        top = pl.multiple_of(first, rows)
        for j in range(NPHI // 2 // 128):
            tab_ref[par, pl.ds(top, rows), j * 128:(j + 1) * 128] = c.astype(jnp.bfloat16)
            tab_ref[par, pl.ds(half + top, rows), j * 128:(j + 1) * 128] = (-s).astype(jnp.bfloat16)
            c, s = c * tc - s * ts, s * tc + c * ts
        return 0

    lax.fori_loop(0, 2 * half // rows, part, 0)


def inverse_order(mode_ref, inv_ref):
    order = lax.broadcasted_iota(jnp.int32, (M, M), 0)
    hit = jnp.where(mode_ref[...] == order, 1.0, 0.0).astype(jnp.bfloat16)
    slot = lax.broadcasted_iota(jnp.int32, (8, M), 1).astype(jnp.float32).astype(jnp.bfloat16)
    found = lax.dot_general(slot, hit, (((1,), (1,)), ((), ())), preferred_element_type=jnp.float32)
    inv_ref[...] = found[:1].astype(jnp.int32)


def relayout(recv_ref, perm_ref, own, block_ref):
    for h in range(2):
        x = jnp.concatenate([recv_ref[4 * h + j].reshape(128, 128) for j in range(4)], axis=1)
        y = jnp.dot(x, perm_ref[...], preferred_element_type=jnp.float32).astype(jnp.bfloat16)
        for q in range(8):
            for i in range(4):
                c, t = divmod(4 * q + i, SLOTS)
                block_ref[own, t, c * SH:(c + 1) * SH, h * 128:(h + 1) * 128] = y[q * SH:(q + 1) * SH, i * 128:(i + 1) * 128]


def fields_kernel(
    mode_hbm, order_hbm, cyc_hbm, norm_hbm, cot_hbm, bes_hbm, out_ref, tab_ref, inv_ref,
    mode_ref, order_ref, cyc_ref, norm_ref, table_ref, cos_ref, sin_ref,
    cot_ref, bes_ref, rad_ref, send_ref, recv_ref, perm_ref, block_ref,
    load_sem, a2a_send, a2a_recv, ring_send, ring_recv,
):
    own = lax.axis_index("blk")
    shell = lax.axis_index("shell")
    core = lax.rem(own, 2)
    x = lax.rem(own // 2, 4)
    z = own // 8
    d = 1 - 2 * core

    def at(dz, k):
        return lax.rem(z + dz, 2) * 8 + lax.rem(x + k * d + 8, 4) * 2 + core

    ahead, behind, across, sibling = at(0, 1), at(0, -1), at(1, 0), own + d

    pairs = [
        (cot_hbm, cot_ref), (bes_hbm, bes_ref), (cyc_hbm, cyc_ref), (norm_hbm, norm_ref), (mode_hbm, mode_ref), (order_hbm, order_ref)
    ]
    loads = [pltpu.make_async_copy(a, b, load_sem.at[i]) for i, (a, b) in enumerate(pairs)]
    for copy in loads:
        copy.start()
    barrier = pltpu.get_barrier_semaphore()
    for peer in (ahead, behind, across, sibling):
        pl.semaphore_signal(barrier, inc=1, device_id={"blk": peer}, device_id_type=MESH)
    for k in range(1, GROUP):
        pl.semaphore_signal(barrier, inc=1, device_id={"shell": lax.rem(shell + k, GROUP)}, device_id_type=MESH)

    for copy in loads[:2]:
        copy.wait()
    radial(cot_ref, bes_ref, rad_ref, send_ref)
    pl.semaphore_wait(barrier, 4 + GROUP - 1)
    exchange = []
    for k in range(1, GROUP):
        to = lax.rem(shell + k, GROUP)
        copy = pltpu.make_async_remote_copy(
            src_ref=send_ref.at[to], dst_ref=recv_ref.at[shell], send_sem=a2a_send.at[k - 1], recv_sem=a2a_recv.at[k - 1],
            device_id={"shell": to}, device_id_type=MESH,
        )
        copy.start()
        exchange.append(copy)
    recv_ref[shell] = send_ref[shell]
    shuffle_matrix(perm_ref)
    for copy in loads[2:]:
        copy.wait()
    cycles = cyc_ref[pl.ds(own, 1), :]
    height = (2.0 * NSIDE - 2.0 * cycles.astype(jnp.float32)) / (3.0 * NSIDE)
    width = 1.0 - height * height
    log_height, slope = jnp.log(width), 2.0 * height * lax.rsqrt(width)
    turn_tables(cycles, cos_ref, sin_ref)
    twiddles(tab_ref)

    def table(block):
        legendre_block(block, log_height, slope, norm_ref, table_ref)

    table(0)
    for k in range(1, GROUP):
        source = lax.rem(shell - k + GROUP, GROUP)
        pltpu.make_async_remote_copy(
            src_ref=send_ref.at[source], dst_ref=recv_ref.at[source], send_sem=a2a_send.at[k - 1], recv_sem=a2a_recv.at[k - 1],
            device_id={"shell": source}, device_id_type=MESH,
        ).wait_recv()
    relayout(recv_ref, perm_ref, own, block_ref)

    sent = []

    def piece(part, index):
        return block_ref.at[index, pl.ds(HALF * part, HALF)]

    def describe(part, index, to, slot):
        return pltpu.make_async_remote_copy(
            src_ref=piece(part, index), dst_ref=piece(part, index), send_sem=ring_send.at[slot],
            recv_sem=ring_recv.at[part, index], device_id={"blk": to}, device_id_type=MESH,
        )

    def send(part, index, *targets):
        for to in targets:
            copy = describe(part, index, to, len(sent))
            copy.start()
            sent.append(copy)

    def arrive(part, index):
        describe(part, index, sibling, 0).wait_recv()

    def slots(*pieces):
        def step(k, _):
            for u in range(4):
                for part, index in pieces:
                    t = HALF * part + k * 4 + u
                    g = index * SLOTS + t
                    re, im = field_of(mode_ref[g], block_ref[index, t], table_ref, cos_ref, sin_ref)
                    out_ref[g, :SH, :] = re
                    out_ref[g, SH:, :] = im
            return 0

        lax.fori_loop(0, HALF // 4, step, 0)

    def both(*pieces):
        other = [(part, index + d) for part, index in pieces]
        for part, index in other:
            arrive(part, index)
        slots(*pieces, *other)

    for part in range(2):
        send(part, own, across, ahead, behind)
    for part in range(2):
        send(part, own, sibling)
    table(3)
    arrive(0, at(1, 0))
    send(0, at(1, 0), ahead, behind)
    arrive(0, at(0, -1))
    send(0, at(0, -1), ahead)
    arrive(0, at(0, 1))
    for index in (at(1, 0), at(0, -1), at(0, 1)):
        send(0, index, sibling)
    table(2)
    arrive(1, at(0, -1))
    send(1, at(0, -1), ahead, across)
    arrive(1, at(0, 1))
    send(1, at(0, 1), across)
    for index in (at(0, -1), at(0, 1)):
        send(1, index, sibling)
    table(1)
    inverse_order(order_ref, inv_ref)
    arrive(0, at(1, -1))
    send(0, at(1, -1), ahead)
    arrive(1, at(0, 2))
    send(1, at(0, 2), across)
    arrive(0, at(0, 2))
    arrive(0, at(1, 1))
    for part, index in ((0, at(1, -1)), (1, at(0, 2)), (0, at(0, 2)), (0, at(1, 1))):
        send(part, index, sibling)
    both((0, own), (1, own))
    both((0, at(1, 0)), (0, at(0, -1)))
    both((0, at(0, 1)), (1, at(0, -1)))
    for index in (at(1, 0), at(1, -1), at(1, 1)):
        arrive(1, index)
        send(1, index, sibling)
    both((1, at(0, 1)), (0, at(1, -1)))
    both((1, at(0, 2)), (0, at(0, 2)))
    arrive(0, at(1, 2))
    send(0, at(1, 2), sibling)
    arrive(1, at(1, 2))
    send(1, at(1, 2), sibling)
    both((0, at(1, 1)), (1, at(1, 0)))
    both((1, at(1, -1)), (1, at(1, 1)))
    both((0, at(1, 2)), (1, at(1, 2)))
    for copy in exchange + sent:
        copy.wait_send()


SPS = 2
JC = 512


def maps_kernel(inv_ref, f_ref, tab_ref, out_ref, g_ref, even_ref, odd_ref):
    half = M // 2
    step = pl.program_id(0)
    last = pl.num_programs(0) - 1

    def sorted_rows(k, _):
        for par in range(2):
            f = jnp.stack([f_ref[inv_ref[0, 32 * k + 2 * u + par]] for u in range(16)])
            for c in range(2):
                w = jnp.transpose(f[:, c * SH:(c + 1) * SH], (1, 0, 2))
                row = pl.multiple_of(par * M + c * half + k * 16, 16)
                for s in range(SH):
                    g_ref[s, pl.ds(row, 16), :] = w[s]
        return 0

    def prepare(first, slot):
        for i in range(SPS):
            even_ref[slot, i * ROWS:(i + 1) * ROWS, :] = g_ref[first + i, :M, :].T
            odd_ref[slot, i * ROWS:(i + 1) * ROWS, :] = g_ref[first + i, M:, :].T

    @pl.when(step == 0)
    def _():
        lax.fori_loop(0, M // 32, sorted_rows, 0)
        prepare(0, 0)

    slot = lax.rem(step, 2)
    even, odd = even_ref[slot], odd_ref[slot]
    prepare(jnp.minimum(step + 1, last) * SPS, 1 - slot)
    for j in range(0, NPHI // 2, JC):
        e = jnp.dot(even, tab_ref[0, :, j:j + JC], preferred_element_type=jnp.float32)
        o = jnp.dot(odd, tab_ref[1, :, j:j + JC], preferred_element_type=jnp.float32)
        p = (e + o).astype(jnp.bfloat16)
        q = (e - o).astype(jnp.bfloat16)
        for i in range(SPS):
            out_ref[i, :, j:j + JC] = p[i * ROWS:(i + 1) * ROWS]
            out_ref[i, :, NPHI // 2 + j:NPHI // 2 + j + JC] = q[i * ROWS:(i + 1) * ROWS]


def maps_call(inverse, fields, table):
    return pl.pallas_call(
        maps_kernel,
        out_shape=jax.ShapeDtypeStruct((SH, ROWS, NPHI), jnp.bfloat16),
        grid=(SH // SPS,),
        in_specs=[
            pl.BlockSpec(memory_space=pltpu.SMEM),
            pl.BlockSpec(memory_space=pltpu.VMEM),
            pl.BlockSpec(memory_space=pltpu.VMEM),
        ],
        out_specs=pl.BlockSpec((SPS, ROWS, NPHI), lambda i: (i, 0, 0)),
        scratch_shapes=[
            pltpu.VMEM((SH, 2 * M, ROWS), jnp.bfloat16),
            pltpu.VMEM((2, SPS * ROWS, M), jnp.bfloat16),
            pltpu.VMEM((2, SPS * ROWS, M), jnp.bfloat16),
        ],
        compiler_params=pltpu.CompilerParams(vmem_limit_bytes=40 << 20),
        name="maps",
    )(inverse, fields, table)


def fields_call(cotangent, bessel, cycle_index, mode_order):
    vmem = pl.BlockSpec(memory_space=pltpu.VMEM)
    hbm = pl.BlockSpec(memory_space=pltpu.HBM)
    return pl.pallas_call(
        fields_kernel,
        out_shape=(
            jax.ShapeDtypeStruct((M, 2 * SH, ROWS), jnp.bfloat16),
            jax.ShapeDtypeStruct((2, M, NPHI // 2), jnp.bfloat16),
            jax.ShapeDtypeStruct((1, M), jnp.int32),
        ),
        in_specs=[hbm] * 6,
        out_specs=(vmem, vmem, vmem),
        scratch_shapes=[
            pltpu.SMEM((M,), jnp.int32),
            pltpu.VMEM((1, M), jnp.int32),
            pltpu.VMEM((16, ROWS), jnp.int32),
            pltpu.VMEM((M, ROWS), jnp.float32),
            pltpu.VMEM((M, L, ROWS), jnp.bfloat16),
            pltpu.VMEM((M, ROWS), jnp.float32),
            pltpu.VMEM((M, ROWS), jnp.float32),
            pltpu.VMEM((2 * SLOTS * KL, WAVES), jnp.float32),
            pltpu.VMEM((KL * WAVES, 128), jnp.float32),
            pltpu.VMEM((2 * SLOTS * KL, 128), jnp.float32),
            pltpu.VMEM((GROUP, 8, SH, 128), jnp.bfloat16),
            pltpu.VMEM((GROUP, 8, SH, 128), jnp.bfloat16),
            pltpu.VMEM((512, 512), jnp.bfloat16),
            pltpu.VMEM((16, SLOTS, 2 * SH, L), jnp.bfloat16),
            pltpu.SemaphoreType.DMA((6,)),
            pltpu.SemaphoreType.DMA((GROUP - 1,)),
            pltpu.SemaphoreType.DMA((GROUP - 1,)),
            pltpu.SemaphoreType.DMA((30,)),
            pltpu.SemaphoreType.DMA((2, 16)),
        ],
        compiler_params=pltpu.CompilerParams(vmem_limit_bytes=48 << 20, collective_id=0, has_side_effects=True),
        name="fields",
    )(
        mode_order, mode_order.reshape(1, -1), cycle_index.reshape(-1, ROWS), jnp.asarray(start_norms()),
        cotangent.reshape(-1, WAVES), bessel.reshape(-1, 128),
    )


def per_device(cotangent, bessel, cycle_index, mode_order):
    fields, table, inverse = fields_call(cotangent, bessel, cycle_index, mode_order)
    return maps_call(inverse, fields, table)


def solution(mesh):
    return jax.shard_map(
        per_device,
        mesh=mesh,
        in_specs=(P(None, "blk", "shell", None), P("shell", None, None), P(), P()),
        out_specs=P("shell", "blk", None),
        check_vma=False,
    )
```

```python
import math

import jax
import jax.numpy as jnp
import numpy as np
from jax import lax
from jax.experimental import pallas as pl
from jax.experimental.pallas import tpu as pltpu
from jax.sharding import PartitionSpec as P

L = 256
M = 256
NSIDE = 1024
NPHI = 4096
ROWS = 128
SH = 16
LB = 64
GROUP = 8
KL = L // GROUP
SLOTS = 16
HALF = SLOTS // 2
WAVES = 128
MESH = pl.DeviceIdType.MESH


def scaled_norms():
    log_gamma = np.array([0.0, 0.0] + [math.lgamma(k) for k in range(2, 2 * L + 1)])
    m, l = np.arange(M)[:, None], np.arange(L)[None, :]
    top = l // LB * LB + LB - 1
    low = np.minimum(m, l)
    log_gain = 0.5 * (
        (l - low) * np.log(top * (top + 1.0)) + log_gamma[l + low + 1] - log_gamma[2 * l + 1] - log_gamma[l - low + 1]
    )
    middle = 0.5 * log_gain[0]
    gain = np.where(m <= l, np.exp(log_gain - middle), 0.0).astype(np.float32)
    start = np.zeros((L, ROWS), np.float32)
    for k in range(L):
        norm = math.log((2 * k + 1) / (4 * math.pi)) + math.lgamma(k + 0.5) - math.lgamma(0.5) - math.lgamma(k + 1.0)
        start[k, 0] = 0.5 * norm + middle[k]
    return start, np.concatenate([gain[:, :ROWS], gain[:, ROWS:]])


def twiddles():
    tables = []
    for parity in range(2):
        m = np.arange(parity, M, 2)[:, None]
        angle = m * np.arange(NPHI // 2)[None, :] % NPHI * (2.0 * math.pi / NPHI)
        w = np.where(m == 0, 2.0 / L, 4.0 / L)
        tables.append(np.concatenate([w * np.cos(angle), -w * np.sin(angle)]))
    return np.stack(tables).astype(np.float32)


def legendre_block(block, log_height, slope, start_ref, table_ref):
    base = block * LB
    groups = LB // 8
    top = base + LB - 1
    c = 1.0 / (top * (top + 1.0))
    sub = lax.broadcasted_iota(jnp.int32, (8, ROWS), 0)
    degrees = [base + 8 * g + sub for g in range(groups)]
    degree_f = [k.astype(jnp.float32) for k in degrees]
    square = [k * (k + 1.0) * c for k in degree_f]
    start = [
        jnp.exp(start_ref[base + 8 * g:base + 8 * g + 8, 0:1] + 0.5 * degree_f[g] * log_height) for g in range(groups)
    ]
    slope = slope * math.sqrt(c)
    unroll = 16

    def clear(i, _):
        for u in range(unroll):
            table_ref[base + LB + i * unroll + u, base:base + LB, :] = jnp.zeros((LB, ROWS), jnp.bfloat16)
        return 0

    lax.fori_loop(0, (M - LB - base) // unroll, clear, 0)

    def descend(first, count, carry, starting):
        def steps(i, carry):
            p, above = carry
            for u in range(unroll):
                m = first - 1 - (i * unroll + u)
                upper = (m + 1).astype(jnp.float32)
                lower = upper * (upper + 1.0) * c
                turn = slope * upper
                new = []
                for g in range(groups):
                    value = turn * p[g] - (square[g] - lower) * above[g]
                    if starting:
                        value = jnp.where(degrees[g] == m, start[g], value)
                    new.append(value)
                for g in range(0, groups, 2):
                    rows = jnp.concatenate([new[g], new[g + 1]], axis=0)
                    table_ref[m, base + 8 * g:base + 8 * g + 16, :] = rows.astype(jnp.bfloat16)
                p, above = new, p
            return p, above

        return lax.fori_loop(0, count // unroll, steps, carry)

    zero = [jnp.zeros((8, ROWS), jnp.float32)] * groups
    carry = descend(base + LB, LB, (zero, zero), True)
    if base:
        descend(base, base, carry, False)


def turn_tables(cycles, cos_ref, sin_ref):
    odd = (lax.rem(cycles + 1, 2) == 1)
    order = lax.broadcasted_iota(jnp.int32, (M, ROWS), 0).astype(jnp.float32)
    a = order * (math.pi / NPHI)
    q = a * a
    cosine = 1.0 - q * (0.5 - q * (1.0 / 24 - q * (1.0 / 720)))
    sine = a * (1.0 - q * (1.0 / 6 - q * (1.0 / 120 - q * (1.0 / 5040))))
    cos_ref[...] = jnp.where(odd, cosine, 1.0)
    sin_ref[...] = jnp.where(odd, sine, 0.0)


def field_of(order, coeffs, table_ref, cos_ref, sin_ref):
    f = jnp.dot(coeffs, table_ref[order], preferred_element_type=jnp.float32)
    c = cos_ref[pl.ds(order, 1), :]
    s = sin_ref[pl.ds(order, 1), :]
    fr, fi = f[:SH], f[SH:]
    return (fr * c - fi * s).astype(jnp.bfloat16), (fr * s + fi * c).astype(jnp.bfloat16)


def radial(group, cot_ref, bes_ref, stage_ref):
    for u in range(8):
        l = group * 8 + u
        c = cot_ref[pl.ds(l, 2 * SLOTS, stride=KL), :].astype(jnp.bfloat16)
        w = bes_ref[l * WAVES:(l + 1) * WAVES, :].astype(jnp.bfloat16)
        stage_ref[pl.ds(l, 2 * SLOTS, stride=KL), :] = jnp.dot(c, w, preferred_element_type=jnp.float32)


def arrange(part, stage_ref, send_ref):
    for n in range(4):
        q = n // 2 * 4 + 2 * part + n % 2
        tile = stage_ref[q * 128:(q + 1) * 128, :].T.astype(jnp.bfloat16)
        for h in range(GROUP):
            send_ref[part, h, n] = tile[h * SH:(h + 1) * SH]


def shuffle_matrix(perm_ref):
    k = lax.broadcasted_iota(jnp.int32, (512, 512), 0)
    n = lax.broadcasted_iota(jnp.int32, (512, 512), 1)
    to = ((k & 96) << 2) | ((k & 384) >> 2) | (k & 31)
    perm_ref[...] = jnp.where(to == n, 1.0, 0.0).astype(jnp.bfloat16)


def inverse_order(mode_ref, inv_ref):
    order = lax.broadcasted_iota(jnp.int32, (M, M), 0)
    hit = jnp.where(mode_ref[...] == order, 1.0, 0.0).astype(jnp.bfloat16)
    slot = lax.broadcasted_iota(jnp.int32, (8, M), 1).astype(jnp.float32).astype(jnp.bfloat16)
    found = lax.dot_general(slot, hit, (((1,), (1,)), ((), ())), preferred_element_type=jnp.float32)
    inv_ref[...] = found[:1].astype(jnp.int32)


def relayout(part, recv_ref, perm_ref, mode_ref, gain_ref, own, block_ref):
    for h in range(2):
        x = jnp.concatenate([recv_ref[part, 4 * h + j].reshape(64, 128) for j in range(4)], axis=1)
        y = jnp.dot(x, perm_ref[...], preferred_element_type=jnp.float32)
        for n in range(4):
            for i in range(4):
                c, t = n // 2, HALF * part + n % 2 * 4 + i
                gain = gain_ref[pl.ds(h * M + mode_ref[own * SLOTS + t], 1), :]
                block = y[n * SH:(n + 1) * SH, i * 128:(i + 1) * 128] * gain
                block_ref[own, t, c * SH:(c + 1) * SH, h * 128:(h + 1) * 128] = block.astype(jnp.bfloat16)


def fields_kernel(
    mode_hbm, order_hbm, cyc_hbm, start_hbm, gain_hbm, wave_hbm, cot_hbm, bes_hbm, out_ref, tab_ref, inv_ref,
    mode_ref, order_ref, cyc_ref, start_ref, gain_ref, table_ref, cos_ref, sin_ref,
    cot_ref, bes_ref, rad_ref, send_ref, recv_ref, perm_ref, block_ref,
    load_sem, a2a_send, a2a_recv, ring_send, ring_recv,
):
    own = lax.axis_index("blk")
    shell = lax.axis_index("shell")
    core = lax.rem(own, 2)
    x = lax.rem(own // 2, 4)
    z = own // 8
    d = 1 - 2 * core

    def at(dz, k):
        return lax.rem(z + dz, 2) * 8 + lax.rem(x + k * d + 8, 4) * 2 + core

    ahead, behind, across, sibling = at(0, 1), at(0, -1), at(1, 0), own + d

    quarter = KL * WAVES // 4
    pairs = [(cot_hbm, cot_ref)]
    pairs += [(bes_hbm.at[pl.ds(k * quarter, quarter)], bes_ref.at[pl.ds(k * quarter, quarter)]) for k in range(4)]
    pairs += [(cyc_hbm, cyc_ref), (start_hbm, start_ref), (mode_hbm, mode_ref), (order_hbm, order_ref), (gain_hbm, gain_ref)]
    pairs += [(wave_hbm, tab_ref)]
    loads = [pltpu.make_async_copy(a, b, load_sem.at[i]) for i, (a, b) in enumerate(pairs)]
    for copy in loads:
        copy.start()
    barrier = pltpu.get_barrier_semaphore()
    for peer in (ahead, behind, across, sibling):
        pl.semaphore_signal(barrier, inc=1, device_id={"blk": peer}, device_id_type=MESH)
    for k in range(1, GROUP):
        pl.semaphore_signal(barrier, inc=1, device_id={"shell": lax.rem(shell + k, GROUP)}, device_id_type=MESH)

    loads[0].wait()
    for k in range(4):
        loads[1 + k].wait()
        radial(k, cot_ref, bes_ref, rad_ref)
    exchange = []
    for part in range(2):
        arrange(part, rad_ref, send_ref)
        if part == 0:
            pl.semaphore_wait(barrier, 4 + GROUP - 1)
        for k in range(1, GROUP):
            to = lax.rem(shell + k, GROUP)
            copy = pltpu.make_async_remote_copy(
                src_ref=send_ref.at[part, to], dst_ref=recv_ref.at[part, shell],
                send_sem=a2a_send.at[part, k - 1], recv_sem=a2a_recv.at[part, k - 1],
                device_id={"shell": to}, device_id_type=MESH,
            )
            copy.start()
            exchange.append(copy)
        recv_ref[part, shell] = send_ref[part, shell]
    shuffle_matrix(perm_ref)
    for copy in loads[5:10]:
        copy.wait()
    cycles = jnp.broadcast_to(cyc_ref[pl.ds(own, 1), :], (8, ROWS))
    height = (2.0 * NSIDE - 2.0 * cycles.astype(jnp.float32)) / (3.0 * NSIDE)
    width = 1.0 - height * height
    log_height, slope = jnp.log(width), 2.0 * height * lax.rsqrt(width)
    turn_tables(cycles[:1], cos_ref, sin_ref)

    def table(block):
        legendre_block(block, log_height, slope, start_ref, table_ref)

    table(0)
    sent = []

    def piece(part, index):
        return block_ref.at[index, pl.ds(HALF * part, HALF)]

    def describe(part, index, to, slot):
        return pltpu.make_async_remote_copy(
            src_ref=piece(part, index), dst_ref=piece(part, index), send_sem=ring_send.at[slot],
            recv_sem=ring_recv.at[part, index], device_id={"blk": to}, device_id_type=MESH,
        )

    def send(part, index, *targets):
        for to in targets:
            copy = describe(part, index, to, len(sent))
            copy.start()
            sent.append(copy)

    def arrive(part, index):
        describe(part, index, sibling, 0).wait_recv()

    def slots(*pieces):
        def step(k, _):
            for u in range(4):
                for part, index in pieces:
                    t = HALF * part + k * 4 + u
                    g = index * SLOTS + t
                    re, im = field_of(mode_ref[g], block_ref[index, t], table_ref, cos_ref, sin_ref)
                    out_ref[g, :SH, :] = re
                    out_ref[g, SH:, :] = im
            return 0

        lax.fori_loop(0, HALF // 4, step, 0)

    def both(*pieces):
        other = [(part, index + d) for part, index in pieces]
        for part, index in other:
            arrive(part, index)
        slots(*pieces, *other)

    for part in range(2):
        for k in range(1, GROUP):
            source = lax.rem(shell - k + GROUP, GROUP)
            pltpu.make_async_remote_copy(
                src_ref=send_ref.at[part, source], dst_ref=recv_ref.at[part, source],
                send_sem=a2a_send.at[part, k - 1], recv_sem=a2a_recv.at[part, k - 1],
                device_id={"shell": source}, device_id_type=MESH,
            ).wait_recv()
        relayout(part, recv_ref, perm_ref, mode_ref, gain_ref, own, block_ref)
        send(part, own, across, ahead, behind)
    for part in range(2):
        send(part, own, sibling)
    table(3)
    arrive(0, at(1, 0))
    send(0, at(1, 0), ahead, behind)
    arrive(0, at(0, -1))
    send(0, at(0, -1), ahead)
    arrive(0, at(0, 1))
    for index in (at(1, 0), at(0, -1), at(0, 1)):
        send(0, index, sibling)
    table(2)
    arrive(1, at(0, -1))
    send(1, at(0, -1), ahead, across)
    arrive(1, at(0, 1))
    send(1, at(0, 1), across)
    for index in (at(0, -1), at(0, 1)):
        send(1, index, sibling)
    table(1)
    inverse_order(order_ref, inv_ref)
    arrive(0, at(1, -1))
    send(0, at(1, -1), ahead)
    arrive(1, at(0, 2))
    send(1, at(0, 2), across)
    arrive(0, at(0, 2))
    arrive(0, at(1, 1))
    for part, index in ((0, at(1, -1)), (1, at(0, 2)), (0, at(0, 2)), (0, at(1, 1))):
        send(part, index, sibling)
    both((0, own), (1, own))
    both((0, at(1, 0)), (0, at(0, -1)))
    both((0, at(0, 1)), (1, at(0, -1)))
    for index in (at(1, 0), at(1, -1), at(1, 1)):
        arrive(1, index)
        send(1, index, sibling)
    both((1, at(0, 1)), (0, at(1, -1)))
    both((1, at(0, 2)), (0, at(0, 2)))
    arrive(0, at(1, 2))
    send(0, at(1, 2), sibling)
    arrive(1, at(1, 2))
    send(1, at(1, 2), sibling)
    both((0, at(1, 1)), (1, at(1, 0)))
    both((1, at(1, -1)), (1, at(1, 1)))
    both((0, at(1, 2)), (1, at(1, 2)))
    for copy in exchange + sent:
        copy.wait_send()
    loads[10].wait()


GROUPS = (2, 4, 4, 4, 2)
JC = 1024


def maps_kernel(inv_ref, f_ref, tab_ref, out_hbm, g_ref, even_ref, odd_ref, map_ref, sem):
    half = M // 2
    firsts = [sum(GROUPS[:i]) for i in range(len(GROUPS))]

    def sorted_rows(k, _):
        for par in range(2):
            f = jnp.stack([f_ref[inv_ref[0, 32 * k + 2 * u + par]] for u in range(16)])
            for c in range(2):
                w = jnp.transpose(f[:, c * SH:(c + 1) * SH], (1, 0, 2))
                row = pl.multiple_of(par * M + c * half + k * 16, 16)
                for s in range(SH):
                    g_ref[s, pl.ds(row, 16), :] = w[s]
        return 0

    def prepare(group):
        for i in range(GROUPS[group]):
            even_ref[group % 2, i * ROWS:(i + 1) * ROWS, :] = g_ref[firsts[group] + i, :M, :].T
            odd_ref[group % 2, i * ROWS:(i + 1) * ROWS, :] = g_ref[firsts[group] + i, M:, :].T

    def copies(group):
        slot = group % 2
        return [
            pltpu.make_async_copy(map_ref.at[slot, i], out_hbm.at[firsts[group] + i], sem.at[slot, i])
            for i in range(GROUPS[group])
        ]

    lax.fori_loop(0, M // 32, sorted_rows, 0)
    prepare(0)
    for group, size in enumerate(GROUPS):
        slot = group % 2
        if group >= 2:
            for copy in copies(group - 2):
                copy.wait()
        if group + 1 < len(GROUPS):
            prepare(group + 1)

        def pixels(k, _):
            low = slice(k * JC, k * JC + JC)
            high = slice(NPHI // 2 + k * JC, NPHI // 2 + k * JC + JC)
            even, odd = even_ref[slot, :size * ROWS, :], odd_ref[slot, :size * ROWS, :]
            e = jnp.dot(even, tab_ref[0, :, low], preferred_element_type=jnp.float32)
            o = jnp.dot(odd, tab_ref[1, :, low], preferred_element_type=jnp.float32)
            map_ref[slot, :size, :, low] = (e + o).astype(jnp.bfloat16).reshape(size, ROWS, JC)
            map_ref[slot, :size, :, high] = (e - o).astype(jnp.bfloat16).reshape(size, ROWS, JC)
            return 0

        for k in range(NPHI // 2 // JC):
            pixels(k, 0)
        for copy in copies(group):
            copy.start()
    for group in range(len(GROUPS) - 2, len(GROUPS)):
        for copy in copies(group):
            copy.wait()


def maps_call(inverse, fields, table):
    most = max(GROUPS)
    return pl.pallas_call(
        maps_kernel,
        out_shape=jax.ShapeDtypeStruct((SH, ROWS, NPHI), jnp.bfloat16),
        in_specs=[
            pl.BlockSpec(memory_space=pltpu.SMEM),
            pl.BlockSpec(memory_space=pltpu.VMEM),
            pl.BlockSpec(memory_space=pltpu.VMEM),
        ],
        out_specs=pl.BlockSpec(memory_space=pl.ANY),
        scratch_shapes=[
            pltpu.VMEM((SH, 2 * M, ROWS), jnp.bfloat16),
            pltpu.VMEM((2, most * ROWS, M), jnp.bfloat16),
            pltpu.VMEM((2, most * ROWS, M), jnp.bfloat16),
            pltpu.VMEM((2, most, ROWS, NPHI), jnp.bfloat16),
            pltpu.SemaphoreType.DMA((2, most)),
        ],
        compiler_params=pltpu.CompilerParams(vmem_limit_bytes=40 << 20),
        name="maps",
    )(inverse, fields, table)


def fields_call(cotangent, bessel, cycle_index, mode_order):
    start, gain = scaled_norms()
    wave = jnp.asarray(twiddles().astype(jnp.bfloat16))
    vmem = pl.BlockSpec(memory_space=pltpu.VMEM)
    hbm = pl.BlockSpec(memory_space=pltpu.HBM)
    return pl.pallas_call(
        fields_kernel,
        out_shape=(
            jax.ShapeDtypeStruct((M, 2 * SH, ROWS), jnp.bfloat16),
            jax.ShapeDtypeStruct((2, M, NPHI // 2), jnp.bfloat16),
            jax.ShapeDtypeStruct((1, M), jnp.int32),
        ),
        in_specs=[hbm] * 8,
        out_specs=(vmem, vmem, vmem),
        scratch_shapes=[
            pltpu.SMEM((M,), jnp.int32),
            pltpu.VMEM((1, M), jnp.int32),
            pltpu.VMEM((16, ROWS), jnp.int32),
            pltpu.VMEM((L, ROWS), jnp.float32),
            pltpu.VMEM((2 * M, ROWS), jnp.float32),
            pltpu.VMEM((M, L, ROWS), jnp.bfloat16),
            pltpu.VMEM((M, ROWS), jnp.float32),
            pltpu.VMEM((M, ROWS), jnp.float32),
            pltpu.VMEM((2 * SLOTS * KL, WAVES), jnp.float32),
            pltpu.VMEM((KL * WAVES, 128), jnp.float32),
            pltpu.VMEM((2 * SLOTS * KL, 128), jnp.float32),
            pltpu.VMEM((2, GROUP, 4, SH, 128), jnp.bfloat16),
            pltpu.VMEM((2, GROUP, 4, SH, 128), jnp.bfloat16),
            pltpu.VMEM((512, 512), jnp.bfloat16),
            pltpu.VMEM((16, SLOTS, 2 * SH, L), jnp.bfloat16),
            pltpu.SemaphoreType.DMA((11,)),
            pltpu.SemaphoreType.DMA((2, GROUP - 1)),
            pltpu.SemaphoreType.DMA((2, GROUP - 1)),
            pltpu.SemaphoreType.DMA((30,)),
            pltpu.SemaphoreType.DMA((2, 16)),
        ],
        compiler_params=pltpu.CompilerParams(vmem_limit_bytes=48 << 20, collective_id=0, has_side_effects=True),
        name="fields",
    )(
        *(
            pltpu.with_memory_space_constraint(a, pltpu.HBM)
            for a in (
                mode_order, mode_order.reshape(1, -1), cycle_index.reshape(-1, ROWS),
                jnp.asarray(start), jnp.asarray(gain), wave,
                cotangent.reshape(-1, WAVES), bessel.reshape(-1, 128),
            )
        )
    )


def per_device(cotangent, bessel, cycle_index, mode_order):
    fields, table, inverse = fields_call(cotangent, bessel, cycle_index, mode_order)
    return maps_call(inverse, fields, table)


def solution(mesh):
    return jax.shard_map(
        per_device,
        mesh=mesh,
        in_specs=(P(None, "blk", "shell", None), P("shell", None, None), P(), P()),
        out_specs=P("shell", "blk", None),
        check_vma=False,
    )
```

```python
import math

import jax
import jax.numpy as jnp
import numpy as np
from jax import lax
from jax.experimental import pallas as pl
from jax.experimental.pallas import tpu as pltpu
from jax.sharding import PartitionSpec as P

L = 256
M = 256
NSIDE = 1024
NPHI = 4096
ROWS = 128
SH = 16
LB = 64
GROUP = 8
KL = L // GROUP
SLOTS = 16
HALF = SLOTS // 2
WAVES = 128
MESH = pl.DeviceIdType.MESH


def scaled_norms():
    log_gamma = np.array([0.0, 0.0] + [math.lgamma(k) for k in range(2, 2 * L + 1)])
    m, l = np.arange(M)[:, None], np.arange(L)[None, :]
    top = l // LB * LB + LB - 1
    low = np.minimum(m, l)
    log_gain = 0.5 * (
        (l - low) * np.log(top * (top + 1.0)) + log_gamma[l + low + 1] - log_gamma[2 * l + 1] - log_gamma[l - low + 1]
    )
    middle = 0.5 * log_gain[0]
    gain = np.where(m <= l, np.exp(log_gain - middle), 0.0).astype(np.float32)
    start = np.zeros((L, ROWS), np.float32)
    for k in range(L):
        norm = math.log((2 * k + 1) / (4 * math.pi)) + math.lgamma(k + 0.5) - math.lgamma(0.5) - math.lgamma(k + 1.0)
        start[k, 0] = 0.5 * norm + middle[k]
    return start, np.concatenate([gain[:, :ROWS], gain[:, ROWS:]])


def twiddles():
    tables = []
    for parity in range(2):
        m = np.arange(parity, M, 2)[:, None]
        angle = m * np.arange(NPHI // 2)[None, :] % NPHI * (2.0 * math.pi / NPHI)
        w = np.where(m == 0, 2.0 / L, 4.0 / L)
        tables.append(np.concatenate([w * np.cos(angle), -w * np.sin(angle)]))
    return np.stack(tables).astype(np.float32)


def legendre_block(block, log_height, slope, start_ref, table_ref):
    base = block * LB
    groups = LB // 8
    top = base + LB - 1
    c = 1.0 / (top * (top + 1.0))
    sub = lax.broadcasted_iota(jnp.int32, (8, ROWS), 0)
    degrees = [base + 8 * g + sub for g in range(groups)]
    degree_f = [k.astype(jnp.float32) for k in degrees]
    square = [k * (k + 1.0) * c for k in degree_f]
    start = [
        jnp.exp(start_ref[base + 8 * g:base + 8 * g + 8, 0:1] + 0.5 * degree_f[g] * log_height) for g in range(groups)
    ]
    slope = slope * math.sqrt(c)
    unroll = 16

    def clear(i, _):
        for u in range(unroll):
            table_ref[base + LB + i * unroll + u, base:base + LB, :] = jnp.zeros((LB, ROWS), jnp.bfloat16)
        return 0

    lax.fori_loop(0, (M - LB - base) // unroll, clear, 0)

    def descend(first, count, carry, starting):
        def steps(i, carry):
            p, above = carry
            for u in range(unroll):
                m = first - 1 - (i * unroll + u)
                upper = (m + 1).astype(jnp.float32)
                lower = upper * (upper + 1.0) * c
                turn = slope * upper
                new = []
                for g in range(groups):
                    value = turn * p[g] - (square[g] - lower) * above[g]
                    if starting:
                        value = jnp.where(degrees[g] == m, start[g], value)
                    new.append(value)
                for g in range(0, groups, 2):
                    rows = jnp.concatenate([new[g], new[g + 1]], axis=0)
                    table_ref[m, base + 8 * g:base + 8 * g + 16, :] = rows.astype(jnp.bfloat16)
                p, above = new, p
            return p, above

        return lax.fori_loop(0, count // unroll, steps, carry)

    zero = [jnp.zeros((8, ROWS), jnp.float32)] * groups
    carry = descend(base + LB, LB, (zero, zero), True)
    if base:
        descend(base, base, carry, False)


def turn_tables(cycles, cos_ref, sin_ref):
    odd = (lax.rem(cycles + 1, 2) == 1)
    order = lax.broadcasted_iota(jnp.int32, (M, ROWS), 0).astype(jnp.float32)
    a = order * (math.pi / NPHI)
    q = a * a
    cosine = 1.0 - q * (0.5 - q * (1.0 / 24 - q * (1.0 / 720)))
    sine = a * (1.0 - q * (1.0 / 6 - q * (1.0 / 120 - q * (1.0 / 5040))))
    cos_ref[...] = jnp.where(odd, cosine, 1.0)
    sin_ref[...] = jnp.where(odd, sine, 0.0)


def field_of(order, coeffs, table_ref, cos_ref, sin_ref):
    f = jnp.dot(coeffs, table_ref[order], preferred_element_type=jnp.float32)
    c = cos_ref[pl.ds(order, 1), :]
    s = sin_ref[pl.ds(order, 1), :]
    fr, fi = f[:SH], f[SH:]
    return (fr * c - fi * s).astype(jnp.bfloat16), (fr * s + fi * c).astype(jnp.bfloat16)


def radial(group, cot_ref, bes_ref, stage_ref):
    for u in range(8):
        l = group * 8 + u
        c = cot_ref[pl.ds(l, 2 * SLOTS, stride=KL), :].astype(jnp.bfloat16)
        w = bes_ref[l * WAVES:(l + 1) * WAVES, :].astype(jnp.bfloat16)
        stage_ref[pl.ds(l, 2 * SLOTS, stride=KL), :] = jnp.dot(c, w, preferred_element_type=jnp.float32)


def arrange(part, stage_ref, send_ref):
    for n in range(4):
        q = n // 2 * 4 + 2 * part + n % 2
        tile = stage_ref[q * 128:(q + 1) * 128, :].T.astype(jnp.bfloat16)
        for h in range(GROUP):
            send_ref[part, h, n] = tile[h * SH:(h + 1) * SH]


def shuffle_matrix(perm_ref):
    k = lax.broadcasted_iota(jnp.int32, (512, 512), 0)
    n = lax.broadcasted_iota(jnp.int32, (512, 512), 1)
    to = ((k & 96) << 2) | ((k & 384) >> 2) | (k & 31)
    perm_ref[...] = jnp.where(to == n, 1.0, 0.0).astype(jnp.bfloat16)


def inverse_order(mode_ref, inv_ref):
    order = lax.broadcasted_iota(jnp.int32, (M, M), 0)
    hit = jnp.where(mode_ref[...] == order, 1.0, 0.0).astype(jnp.bfloat16)
    slot = lax.broadcasted_iota(jnp.int32, (8, M), 1).astype(jnp.float32).astype(jnp.bfloat16)
    found = lax.dot_general(slot, hit, (((1,), (1,)), ((), ())), preferred_element_type=jnp.float32)
    inv_ref[...] = found[:1].astype(jnp.int32)


def relayout(part, recv_ref, perm_ref, mode_ref, gain_ref, own, block_ref):
    for h in range(2):
        x = jnp.concatenate([recv_ref[part, 4 * h + j].reshape(64, 128) for j in range(4)], axis=1)
        y = jnp.dot(x, perm_ref[...], preferred_element_type=jnp.float32)
        for n in range(4):
            for i in range(4):
                c, t = n // 2, HALF * part + n % 2 * 4 + i
                gain = gain_ref[pl.ds(h * M + mode_ref[own * SLOTS + t], 1), :]
                block = y[n * SH:(n + 1) * SH, i * 128:(i + 1) * 128] * gain
                block_ref[own, t, c * SH:(c + 1) * SH, h * 128:(h + 1) * 128] = block.astype(jnp.bfloat16)


def fields_kernel(
    mode_hbm, order_hbm, cyc_hbm, start_hbm, gain_hbm, wave_hbm, cot_hbm, bes_hbm, out_ref, tab_ref, inv_ref,
    mode_ref, order_ref, cyc_ref, start_ref, gain_ref, table_ref, cos_ref, sin_ref,
    cot_ref, bes_ref, rad_ref, send_ref, recv_ref, perm_ref, block_ref,
    load_sem, a2a_send, a2a_recv, ring_send, ring_recv,
):
    own = lax.axis_index("blk")
    shell = lax.axis_index("shell")
    core = lax.rem(own, 2)
    x = lax.rem(own // 2, 4)
    z = own // 8
    d = 1 - 2 * core

    def at(dz, k):
        return lax.rem(z + dz, 2) * 8 + lax.rem(x + k * d + 8, 4) * 2 + core

    ahead, behind, across, sibling = at(0, 1), at(0, -1), at(1, 0), own + d

    quarter = KL * WAVES // 4
    pairs = [(cot_hbm, cot_ref.at[pl.ds(0, 2 * SLOTS * KL)])]
    pairs += [(bes_hbm.at[pl.ds(k * quarter, quarter)], bes_ref.at[pl.ds(k * quarter, quarter)]) for k in range(4)]
    pairs += [(cyc_hbm, cyc_ref), (start_hbm, start_ref), (mode_hbm, mode_ref), (order_hbm, order_ref), (gain_hbm, gain_ref)]
    pairs += [(wave_hbm, tab_ref)]
    loads = [pltpu.make_async_copy(a, b, load_sem.at[i]) for i, (a, b) in enumerate(pairs)]
    for copy in loads:
        copy.start()
    barrier = pltpu.get_barrier_semaphore()
    for peer in (ahead, behind, across, sibling):
        pl.semaphore_signal(barrier, inc=1, device_id={"blk": peer}, device_id_type=MESH)
    for k in range(1, GROUP):
        pl.semaphore_signal(barrier, inc=1, device_id={"shell": lax.rem(shell + k, GROUP)}, device_id_type=MESH)

    loads[0].wait()
    for k in range(4):
        loads[1 + k].wait()
        radial(k, cot_ref, bes_ref, rad_ref)
    exchange = []
    for part in range(2):
        arrange(part, rad_ref, send_ref)
        if part == 0:
            pl.semaphore_wait(barrier, 4 + GROUP - 1)
        for k in range(1, GROUP):
            to = lax.rem(shell + k, GROUP)
            copy = pltpu.make_async_remote_copy(
                src_ref=send_ref.at[part, to], dst_ref=recv_ref.at[part, shell],
                send_sem=a2a_send.at[part, k - 1], recv_sem=a2a_recv.at[part, k - 1],
                device_id={"shell": to}, device_id_type=MESH,
            )
            copy.start()
            exchange.append(copy)
        recv_ref[part, shell] = send_ref[part, shell]
    shuffle_matrix(perm_ref)
    for copy in loads[5:10]:
        copy.wait()
    cycles = jnp.broadcast_to(cyc_ref[pl.ds(own, 1), :], (8, ROWS))
    height = (2.0 * NSIDE - 2.0 * cycles.astype(jnp.float32)) / (3.0 * NSIDE)
    width = 1.0 - height * height
    log_height, slope = jnp.log(width), 2.0 * height * lax.rsqrt(width)
    turn_tables(cycles[:1], cos_ref, sin_ref)

    def table(block):
        legendre_block(block, log_height, slope, start_ref, table_ref)

    table(0)
    sent = []

    def piece(part, index):
        return block_ref.at[index, pl.ds(HALF * part, HALF)]

    def describe(part, index, to, slot):
        return pltpu.make_async_remote_copy(
            src_ref=piece(part, index), dst_ref=piece(part, index), send_sem=ring_send.at[slot],
            recv_sem=ring_recv.at[part, index], device_id={"blk": to}, device_id_type=MESH,
        )

    def send(part, index, *targets):
        for to in targets:
            copy = describe(part, index, to, len(sent))
            copy.start()
            sent.append(copy)

    def arrive(part, index):
        describe(part, index, sibling, 0).wait_recv()

    def slots(*pieces):
        def step(k, _):
            for u in range(4):
                for part, index in pieces:
                    t = HALF * part + k * 4 + u
                    g = index * SLOTS + t
                    re, im = field_of(mode_ref[g], block_ref[index, t], table_ref, cos_ref, sin_ref)
                    out_ref[g, :SH, :] = re
                    out_ref[g, SH:, :] = im
            return 0

        lax.fori_loop(0, HALF // 4, step, 0)

    def both(*pieces):
        other = [(part, index + d) for part, index in pieces]
        for part, index in other:
            arrive(part, index)
        slots(*pieces, *other)

    for part in range(2):
        for k in range(1, GROUP):
            source = lax.rem(shell - k + GROUP, GROUP)
            pltpu.make_async_remote_copy(
                src_ref=send_ref.at[part, source], dst_ref=recv_ref.at[part, source],
                send_sem=a2a_send.at[part, k - 1], recv_sem=a2a_recv.at[part, k - 1],
                device_id={"shell": source}, device_id_type=MESH,
            ).wait_recv()
        relayout(part, recv_ref, perm_ref, mode_ref, gain_ref, own, block_ref)
        send(part, own, across, ahead, behind)
    for part in range(2):
        send(part, own, sibling)
    table(3)
    arrive(0, at(1, 0))
    send(0, at(1, 0), ahead, behind)
    arrive(0, at(0, -1))
    send(0, at(0, -1), ahead)
    arrive(0, at(0, 1))
    for index in (at(1, 0), at(0, -1), at(0, 1)):
        send(0, index, sibling)
    table(2)
    arrive(1, at(0, -1))
    send(1, at(0, -1), ahead, across)
    arrive(1, at(0, 1))
    send(1, at(0, 1), across)
    for index in (at(0, -1), at(0, 1)):
        send(1, index, sibling)
    table(1)
    inverse_order(order_ref, inv_ref)
    arrive(0, at(1, -1))
    send(0, at(1, -1), ahead)
    arrive(1, at(0, 2))
    send(1, at(0, 2), across)
    arrive(0, at(0, 2))
    arrive(0, at(1, 1))
    for part, index in ((0, at(1, -1)), (1, at(0, 2)), (0, at(0, 2)), (0, at(1, 1))):
        send(part, index, sibling)
    both((0, own), (1, own))
    both((0, at(1, 0)), (0, at(0, -1)))
    both((0, at(0, 1)), (1, at(0, -1)))
    for index in (at(1, 0), at(1, -1), at(1, 1)):
        arrive(1, index)
        send(1, index, sibling)
    both((1, at(0, 1)), (0, at(1, -1)))
    both((1, at(0, 2)), (0, at(0, 2)))
    arrive(0, at(1, 2))
    send(0, at(1, 2), sibling)
    arrive(1, at(1, 2))
    send(1, at(1, 2), sibling)
    both((0, at(1, 1)), (1, at(1, 0)))
    both((1, at(1, -1)), (1, at(1, 1)))
    both((0, at(1, 2)), (1, at(1, 2)))
    for copy in exchange + sent:
        copy.wait_send()
    loads[10].wait()


GROUPS = (2, 4, 4, 4, 2)
JC = 1024


def maps_kernel(inv_ref, f_ref, tab_ref, out_hbm, g_ref, even_ref, odd_ref, map_ref, sem):
    half = M // 2
    firsts = [sum(GROUPS[:i]) for i in range(len(GROUPS))]

    def sorted_rows(k, _):
        for par in range(2):
            f = jnp.stack([f_ref[inv_ref[0, 32 * k + 2 * u + par]] for u in range(16)])
            for c in range(2):
                w = jnp.transpose(f[:, c * SH:(c + 1) * SH], (1, 0, 2))
                row = pl.multiple_of(par * M + c * half + k * 16, 16)
                for s in range(SH):
                    g_ref[s, pl.ds(row, 16), :] = w[s]
        return 0

    def prepare(group):
        for i in range(GROUPS[group]):
            even_ref[group % 2, i * ROWS:(i + 1) * ROWS, :] = g_ref[firsts[group] + i, :M, :].T
            odd_ref[group % 2, i * ROWS:(i + 1) * ROWS, :] = g_ref[firsts[group] + i, M:, :].T

    def copies(group):
        slot = group % 2
        return [
            pltpu.make_async_copy(map_ref.at[slot, i], out_hbm.at[firsts[group] + i], sem.at[slot, i])
            for i in range(GROUPS[group])
        ]

    lax.fori_loop(0, M // 32, sorted_rows, 0)
    prepare(0)
    for group, size in enumerate(GROUPS):
        slot = group % 2
        if group >= 2:
            for copy in copies(group - 2):
                copy.wait()
        if group + 1 < len(GROUPS):
            prepare(group + 1)

        def pixels(k, _):
            low = slice(k * JC, k * JC + JC)
            high = slice(NPHI // 2 + k * JC, NPHI // 2 + k * JC + JC)
            even, odd = even_ref[slot, :size * ROWS, :], odd_ref[slot, :size * ROWS, :]
            e = jnp.dot(even, tab_ref[0, :, low], preferred_element_type=jnp.float32)
            o = jnp.dot(odd, tab_ref[1, :, low], preferred_element_type=jnp.float32)
            map_ref[slot, :size, :, low] = (e + o).astype(jnp.bfloat16).reshape(size, ROWS, JC)
            map_ref[slot, :size, :, high] = (e - o).astype(jnp.bfloat16).reshape(size, ROWS, JC)
            return 0

        for k in range(NPHI // 2 // JC):
            pixels(k, 0)
        for copy in copies(group):
            copy.start()
    for group in range(len(GROUPS) - 2, len(GROUPS)):
        for copy in copies(group):
            copy.wait()


def maps_call(inverse, fields, table):
    most = max(GROUPS)
    return pl.pallas_call(
        maps_kernel,
        out_shape=jax.ShapeDtypeStruct((SH, ROWS, NPHI), jnp.bfloat16),
        in_specs=[
            pl.BlockSpec(memory_space=pltpu.SMEM),
            pl.BlockSpec(memory_space=pltpu.VMEM),
            pl.BlockSpec(memory_space=pltpu.VMEM),
        ],
        out_specs=pl.BlockSpec(memory_space=pl.ANY),
        scratch_shapes=[
            pltpu.VMEM((SH, 2 * M, ROWS), jnp.bfloat16),
            pltpu.VMEM((2, most * ROWS, M), jnp.bfloat16),
            pltpu.VMEM((2, most * ROWS, M), jnp.bfloat16),
            pltpu.VMEM((2, most, ROWS, NPHI), jnp.bfloat16),
            pltpu.SemaphoreType.DMA((2, most)),
        ],
        compiler_params=pltpu.CompilerParams(vmem_limit_bytes=40 << 20),
        name="maps",
    )(inverse, fields, table)


def fields_call(cotangent, bessel, cycle_index, mode_order):
    start, gain = scaled_norms()
    wave = jnp.asarray(twiddles().astype(jnp.bfloat16))
    vmem = pl.BlockSpec(memory_space=pltpu.VMEM)
    hbm = pl.BlockSpec(memory_space=pltpu.HBM)
    return pl.pallas_call(
        fields_kernel,
        out_shape=(
            jax.ShapeDtypeStruct((M, 2 * SH, ROWS), jnp.bfloat16),
            jax.ShapeDtypeStruct((2, M, NPHI // 2), jnp.bfloat16),
            jax.ShapeDtypeStruct((1, M), jnp.int32),
        ),
        in_specs=[hbm] * 8,
        out_specs=(vmem, vmem, vmem),
        scratch_shapes=[
            pltpu.SMEM((M,), jnp.int32),
            pltpu.VMEM((1, M), jnp.int32),
            pltpu.VMEM((16, ROWS), jnp.int32),
            pltpu.VMEM((L, ROWS), jnp.float32),
            pltpu.VMEM((2 * M, ROWS), jnp.float32),
            pltpu.VMEM((M, L, ROWS), jnp.bfloat16),
            pltpu.VMEM((M, ROWS), jnp.float32),
            pltpu.VMEM((M, ROWS), jnp.float32),
            pltpu.VMEM((2 * SLOTS * KL + KL, WAVES), jnp.float32),
            pltpu.VMEM((KL * WAVES, 128), jnp.float32),
            pltpu.VMEM((2 * SLOTS * KL + KL, 128), jnp.float32),
            pltpu.VMEM((2, GROUP, 4, SH, 128), jnp.bfloat16),
            pltpu.VMEM((2, GROUP, 4, SH, 128), jnp.bfloat16),
            pltpu.VMEM((512, 512), jnp.bfloat16),
            pltpu.VMEM((16, SLOTS, 2 * SH, L), jnp.bfloat16),
            pltpu.SemaphoreType.DMA((11,)),
            pltpu.SemaphoreType.DMA((2, GROUP - 1)),
            pltpu.SemaphoreType.DMA((2, GROUP - 1)),
            pltpu.SemaphoreType.DMA((30,)),
            pltpu.SemaphoreType.DMA((2, 16)),
        ],
        compiler_params=pltpu.CompilerParams(vmem_limit_bytes=48 << 20, collective_id=0, has_side_effects=True),
        name="fields",
    )(
        *(
            pltpu.with_memory_space_constraint(a, pltpu.HBM)
            for a in (
                mode_order, mode_order.reshape(1, -1), cycle_index.reshape(-1, ROWS),
                jnp.asarray(start), jnp.asarray(gain), wave,
                cotangent.reshape(-1, WAVES), bessel.reshape(-1, 128),
            )
        )
    )


def per_device(cotangent, bessel, cycle_index, mode_order):
    fields, table, inverse = fields_call(cotangent, bessel, cycle_index, mode_order)
    return maps_call(inverse, fields, table)


def solution(mesh):
    return jax.shard_map(
        per_device,
        mesh=mesh,
        in_specs=(P(None, "blk", "shell", None), P("shell", None, None), P(), P()),
        out_specs=P("shell", "blk", None),
        check_vma=False,
    )
```
